32 devices in a mesh: dp: 4 (over x, core), expert: 8 (over z, y).
Axes of the slice: x: 2, y: 2, z: 4, core: 2. Of those that a mesh axis runs over, the one named last changes fastest.
Arguments:
- tokens: bfloat16 [4, 1024, 2048], P('dp', 'expert'), may hold values from -6 to 6
- cotangent: bfloat16 [4, 1024, 2048], P('dp', 'expert'), may hold values from -0.796875 to 0.796875
- w_gate: bfloat16 [8, 2048, 384], P('expert'), may hold values from -0.125 to 0.125
- w_up: bfloat16 [8, 2048, 384], P('expert'), may hold values from -0.125 to 0.125
- w_down: bfloat16 [8, 384, 2048], P('expert'), may hold values from -0.3125 to 0.3125
- route_owner: int32 [4, 8, 256], P('dp'), may hold values from 0 to 7, as said below
- route_row: int32 [4, 8, 256], P('dp'), may hold values from 0 to 127
- gates: float32 [4, 8, 256], P('dp', 'expert'), may hold values from 0.1 to 1
Outputs:
- token_grads: bfloat16 [4, 1024, 2048], P('dp', 'expert')
- grad_gate: float32 [8, 2048, 384], P('expert', 'dp')
- grad_up: float32 [8, 2048, 384], P('expert', 'dp')
- grad_down: float32 [8, 384, 2048], P('expert', None, 'dp')
- gate_grads: float32 [4, 8, 256], P('dp', 'expert')
The draws below stay inside these ranges and needn't reach their ends.
Inputs may be any that keep to these rules, and one draw needn't show every extreme that they name: Within one group and expert no (route_owner, route_row) pair repeats; an expert takes at most 40 tokens of one device, and exactly 40 of at least one device.
All inputs are finite; a program needn't handle non-finite values.
Results may differ from the reference program's by a relative error of at most 0.008.
Values may be sent and summed in bfloat16 or wider, within the bound.
A program may use at most 64 MiB of HBM per device.

```python
import math
import jax
import jax.numpy as jnp
from jax import lax

D = 2048
FF = 384
TOK_DEV = 128
OWNERS = 8
EXPERTS = 8
GROUPS = 4
TOKENS_G = 1024
C = 256
CAP = 40


def routing_pairs(key):
    slots_total = OWNERS * CAP

    def one_expert(expert_key):
        first_key, second_key, third_key = jax.random.split(expert_key, 3)
        full_owner = jax.random.randint(first_key, (), 0, OWNERS)
        priority = jax.random.permutation(second_key, slots_total)
        owner_of = jnp.arange(slots_total) // CAP
        priority = jnp.where(owner_of == full_owner, priority - slots_total, priority)
        chosen = jnp.argsort(priority, stable=True)[:C]
        row_keys = jax.random.split(third_key, OWNERS)
        row_table = jax.vmap(lambda row_key: jax.random.permutation(row_key, TOK_DEV)[:CAP])(row_keys)
        return ((chosen // CAP).astype(jnp.int32), row_table.reshape(-1)[chosen].astype(jnp.int32))
    expert_keys = jax.random.split(key, GROUPS * EXPERTS)
    owner_ids, row_ids = jax.vmap(one_expert)(expert_keys)
    return (owner_ids.reshape(GROUPS, EXPERTS, C), row_ids.reshape(GROUPS, EXPERTS, C))


def draw_route_owner(key, part):
    return routing_pairs(key)[0]


def draw_route_row(key, part):
    return routing_pairs(key)[1]


def strengthened(entries, key, source, target, blocks, factor):
    owner, partner = [(jnp.arange(entries.shape[dim]) // (entries.shape[dim] // blocks)).reshape([-1 if axis == dim else 1 for axis in range(entries.ndim)]) for dim in (source, target)]
    chosen = jax.random.permutation(key, blocks)[partner]
    strong = (owner == chosen) | (owner == (partner + blocks // 2) % blocks)
    return jnp.where(strong, factor * entries, entries)


def levels(own_key, shape, pieces, low, largest):
    def one(axis_at, blocks):
        steps = jax.random.uniform(jax.random.fold_in(jax.random.fold_in(own_key, 6), axis_at), (blocks,), jnp.float32, low / len(pieces), largest / len(pieces))
        return jnp.repeat(jnp.exp(steps), shape[axis_at] // blocks).reshape((-1,) + (1,) * (len(shape) - axis_at - 1))

    level = one(*pieces[0])
    for cut in pieces[1:]:
        level = level * one(*cut)
    return level


def gaussian(own_key, shape, width, reach, shards=(), dtype=jnp.bfloat16):
    array = width * jax.random.normal(own_key, shape, jnp.float32)
    if shards:
        array = array * levels(own_key, shape, shards, -0.22, 0.18)
    return jnp.clip(array, -reach, reach).astype(dtype)


def noise_with(stream_key, dims, spread, limit, pieces, heavy, held_as=jnp.bfloat16):
    array = spread * jax.random.normal(stream_key, dims, jnp.float32)
    if pieces:
        array = array * levels(stream_key, dims, pieces, -0.22, 0.18)
    return jnp.clip(strengthened(array, jax.random.fold_in(stream_key, 3), *heavy), -limit, limit).astype(held_as)


def setup_inputs(seed: int = 0) -> dict:
    splits = jax.random.split(jax.random.key(seed), 9)
    tokens = gaussian(splits[0], (GROUPS, TOKENS_G, D), 1.0, 6.0, ((0, 4), (1, 8)))
    cotangent = noise_with(splits[1], (GROUPS, TOKENS_G, D), 0.1, 0.796875, ((0, 4), (1, 8)), (0, 2, 4, 2.0))
    w_gate = gaussian(splits[2], (EXPERTS, D, FF), D ** -0.5, 0.125, ((0, 8),))
    w_up = gaussian(splits[3], (EXPERTS, D, FF), D ** -0.5, 0.125, ((0, 8),))
    w_down = gaussian(splits[4], (EXPERTS, FF, D), FF ** -0.5, 0.3125, ((0, 8),))
    route_owner = draw_route_owner(jax.random.fold_in(splits[8], 71), 0)
    route_row = draw_route_row(jax.random.fold_in(splits[8], 71), 0)
    gates = jnp.clip(jnp.exp(math.log(1.0) - 2.3025851 * jax.random.uniform(splits[7], (GROUPS, EXPERTS, C), jnp.float32) ** levels(splits[7], (GROUPS, EXPERTS, C), ((0, 4), (1, 8)), -0.2, 0.2)), 0.1, 1.0)
    return dict(tokens=tokens, cotangent=cotangent, w_gate=w_gate, w_up=w_up, w_down=w_down, route_owner=route_owner, route_row=route_row, gates=gates)


def select_rows(table, positions):
    return table[positions]


def add_rows(total, positions, values):
    return total.at[positions].add(values.astype(jnp.float32))


def group_sum(left, right, form):
    parts = jnp.einsum(form, left.reshape(GROUPS, C, -1).astype(jnp.float32), right.reshape(GROUPS, C, -1).astype(jnp.float32))
    rounded = lax.optimization_barrier(parts.astype(jnp.bfloat16))
    return jnp.sum(rounded.astype(jnp.float32), axis=0)


def reference(tokens, cotangent, w_gate, w_up, w_down, route_owner, route_row, gates):
    def backward_one(carry, inputs):
        gate_matrix, up_matrix, down_matrix, owner_ids, row_ids, weights = inputs
        positions = (owner_ids * TOK_DEV + row_ids).astype(jnp.int32)
        flat_in = jax.vmap(select_rows)(tokens, positions).reshape(GROUPS * C, D)
        flat_out = jax.vmap(select_rows)(cotangent, positions).reshape(GROUPS * C, D)
        pre_gate = jnp.dot(flat_in, gate_matrix, preferred_element_type=jnp.float32)
        pre_up = jnp.dot(flat_in, up_matrix, preferred_element_type=jnp.float32)
        sigma = jax.nn.sigmoid(pre_gate)
        activated = pre_gate * sigma
        hidden = (activated * pre_up).astype(jnp.bfloat16)
        expert_out = jnp.dot(hidden, down_matrix, preferred_element_type=jnp.float32)
        gate_grad = jnp.sum(flat_out.astype(jnp.float32) * expert_out, axis=1)
        scaled = (weights.reshape(-1)[:, None] * flat_out.astype(jnp.float32)).astype(jnp.bfloat16)
        d_hidden = jnp.dot(scaled, down_matrix.T, preferred_element_type=jnp.float32)
        d_pre_gate = (d_hidden * pre_up * sigma * (1.0 + pre_gate * (1.0 - sigma))).astype(jnp.bfloat16)
        d_pre_up = (d_hidden * activated).astype(jnp.bfloat16)
        row_grad = (jnp.dot(d_pre_gate, gate_matrix.T, preferred_element_type=jnp.float32)
                    + jnp.dot(d_pre_up, up_matrix.T, preferred_element_type=jnp.float32)).astype(jnp.bfloat16)
        carry = jax.vmap(add_rows)(carry, positions, row_grad.reshape(GROUPS, C, D))
        grad_gate = group_sum(flat_in, d_pre_gate, "gcd,gcf->gdf")
        grad_up = group_sum(flat_in, d_pre_up, "gcd,gcf->gdf")
        grad_down = group_sum(hidden, scaled, "gcf,gcd->gfd")
        return carry, (grad_gate, grad_up, grad_down, gate_grad.reshape(GROUPS, C))

    start = jnp.zeros((GROUPS, TOKENS_G, D), jnp.float32)
    scan_inputs = (w_gate, w_up, w_down, route_owner.transpose(1, 0, 2), route_row.transpose(1, 0, 2), gates.transpose(1, 0, 2))
    total, outputs = lax.scan(backward_one, start, scan_inputs)
    grad_gate, grad_up, grad_down, gate_grads = outputs
    return total.astype(jnp.bfloat16), grad_gate, grad_up, grad_down, gate_grads.transpose(1, 0, 2)
```

```python
import functools

import jax
import jax.numpy as jnp
from jax import lax
from jax.experimental import pallas as pl
from jax.experimental.pallas import tpu as pltpu
from jax.sharding import PartitionSpec as P


def contract_first(left, right):
    return lax.dot_general(
        left, right, (((0,), (0,)), ((), ())), preferred_element_type=jnp.float32
    )


def contract_last(left, right):
    return lax.dot_general(
        left, right, (((1,), (1,)), ((), ())), preferred_element_type=jnp.float32
    )


def on_device(tokens, cotangent, w_gate, w_up, w_down, route_owner, route_row, gates):
    peers = lax.axis_size("expert")
    device = lax.axis_index("expert")
    local_tokens = tokens[0]
    local_cotangent = cotangent[0]
    gate_matrix = w_gate[0]
    up_matrix = w_up[0]
    down_matrix = w_down[0]
    owners_all = route_owner[0]
    rows_all = route_row[0]
    token_count = local_tokens.shape[0]
    width = local_tokens.shape[1]
    slots_each = owners_all.shape[1]
    capacity = (5 * slots_each + 4 * peers - 1) // (4 * peers)
    held_here = owners_all == device
    ranks_here = jnp.cumsum(held_here.astype(jnp.int32), axis=1) - 1
    levels = jnp.arange(capacity, dtype=jnp.int32)
    matches = held_here[None, :, :] & (ranks_here[None, :, :] == levels[:, None, None])
    wanted_by_level = jnp.sum(jnp.where(matches, rows_all[None, :, :] + 1, 0), axis=2) - 1
    wanted = wanted_by_level.T.reshape(-1)
    selector = (wanted[:, None] == jnp.arange(token_count, dtype=jnp.int32)[None, :]).astype(
        jnp.bfloat16
    )
    send_inputs = jnp.dot(selector, local_tokens, preferred_element_type=jnp.float32).astype(
        jnp.bfloat16
    )
    send_outputs = jnp.dot(selector, local_cotangent, preferred_element_type=jnp.float32).astype(
        jnp.bfloat16
    )
    got_inputs = lax.all_to_all(
        send_inputs.reshape(peers, capacity * width),
        "expert",
        split_axis=0,
        concat_axis=0,
        tiled=True,
    )
    got_outputs = lax.all_to_all(
        send_outputs.reshape(peers, capacity * width),
        "expert",
        split_axis=0,
        concat_axis=0,
        tiled=True,
    )
    own_owner = lax.dynamic_index_in_dim(owners_all, device, 0, keepdims=False)
    own_gate = gates[0, 0]
    owner_hits = (own_owner[:, None] == jnp.arange(peers, dtype=jnp.int32)[None, :]).astype(
        jnp.int32
    )
    own_rank = jnp.sum(owner_hits * (jnp.cumsum(owner_hits, axis=0) - 1), axis=1)
    slot_index = own_owner * capacity + own_rank
    flat_inputs = got_inputs.reshape(peers * capacity, width)
    flat_outputs = got_outputs.reshape(peers * capacity, width)
    rows_in = jnp.take(flat_inputs, slot_index, axis=0)
    rows_out = jnp.take(flat_outputs, slot_index, axis=0)
    pre_gate = jnp.dot(rows_in, gate_matrix, preferred_element_type=jnp.float32)
    pre_up = jnp.dot(rows_in, up_matrix, preferred_element_type=jnp.float32)
    sigma = jax.nn.sigmoid(pre_gate)
    activated = pre_gate * sigma
    hidden = (activated * pre_up).astype(jnp.bfloat16)
    expert_out = jnp.dot(hidden, down_matrix, preferred_element_type=jnp.float32)
    gate_grad_rows = jnp.sum(rows_out.astype(jnp.float32) * expert_out, axis=1)
    scaled = (own_gate[:, None] * rows_out.astype(jnp.float32)).astype(jnp.bfloat16)
    d_hidden = contract_last(scaled, down_matrix)
    d_pre_gate = (d_hidden * pre_up * sigma * (1.0 + pre_gate * (1.0 - sigma))).astype(jnp.bfloat16)
    d_pre_up = (d_hidden * activated).astype(jnp.bfloat16)
    row_grad = (contract_last(d_pre_gate, gate_matrix) + contract_last(d_pre_up, up_matrix)).astype(
        jnp.bfloat16
    )
    gate_part = contract_first(rows_in, d_pre_gate)
    up_part = contract_first(rows_in, d_pre_up)
    down_part = contract_first(scaled, hidden)
    gate_sum, up_sum, down_sum = (
        lax.psum_scatter(
            gate_part.astype(jnp.bfloat16), "dp", scatter_dimension=0, tiled=True
        ).astype(jnp.float32),
        lax.psum_scatter(
            up_part.astype(jnp.bfloat16), "dp", scatter_dimension=0, tiled=True
        ).astype(jnp.float32),
        lax.psum_scatter(
            down_part.astype(jnp.bfloat16), "dp", scatter_dimension=0, tiled=True
        ).astype(jnp.float32),
    )
    back_rows = jnp.zeros((peers * capacity, width), jnp.bfloat16).at[slot_index].set(row_grad)
    got_back = lax.all_to_all(
        back_rows.reshape(peers, capacity * width),
        "expert",
        split_axis=0,
        concat_axis=0,
        tiled=True,
    )
    token_grads = contract_first(selector, got_back.reshape(peers * capacity, width)).astype(
        jnp.bfloat16
    )
    return (
        token_grads[None],
        gate_sum[None],
        up_sum[None],
        down_sum.T[None],
        gate_grad_rows[None, None],
    )


MESH = pl.DeviceIdType.MESH
F32 = jnp.float32
BF16 = jnp.bfloat16
ORDER = (6, 7, 4, 5, 2, 3, 1)


def flipped(index, bits, size):
    out = 0
    step = 1
    while step < size:
        out = out + step * (((index // step) % 2 + (bits // step) % 2) % 2)
        step *= 2
    return out


def dot(left, right):
    return jnp.dot(left, right, preferred_element_type=F32)


def fused(
    peers, cap, tok_hbm, cot_hbm, wg_hbm, wu_hbm, wd_hbm, owner_ref, row_ref, gates_ref,
    tg_out, gg_out, gu_out, gd_out, gr_out,
    tt, cc, wgu, wd, code_ref, sel, put, take, send, got, back_send, back_got,
    rows, pre, dpre, hid, outg,
    core_send_a, core_got_a, own_a, x_send_a, x_got_a,
    core_send_b, core_got_b, own_b, x_send_b, x_got_b,
    load_sem, send_sem, recv_sem, bsend_sem, brecv_sem, csend_sem, crecv_sem, xsend_sem, xrecv_sem,
):
    me = lax.axis_index("expert")
    dp = lax.axis_index("dp")
    plane, core = dp // 2, dp % 2
    sibling = plane * 2 + (1 - core)
    across = (1 - plane) * 2 + core
    tokens_here, width = tok_hbm.shape
    half = width // 2
    slots = owner_ref.shape[1]
    ff = wg_hbm.shape[1]
    shard = width // 4
    slab = 2 * cap
    partners = {k: flipped(me, k, peers) for k in range(peers)}

    loads = []
    for number, (src, dst) in enumerate((
        (tok_hbm.at[:, pl.ds(0, half)], tt.at[pl.ds(0, tokens_here)]),
        (tok_hbm.at[:, pl.ds(half, half)], tt.at[pl.ds(tokens_here, tokens_here)]),
        (cot_hbm.at[:, pl.ds(0, half)], cc.at[pl.ds(0, tokens_here)]),
        (cot_hbm.at[:, pl.ds(half, half)], cc.at[pl.ds(tokens_here, tokens_here)]),
        (wg_hbm, wgu.at[:, pl.ds(0, ff)]),
        (wu_hbm, wgu.at[:, pl.ds(ff, ff)]),
        (wd_hbm, wd),
    )):
        copy = pltpu.make_async_copy(src, dst, load_sem.at[number])
        copy.start()
        loads.append(copy)

    barrier = pltpu.get_barrier_semaphore()
    for k in ORDER:
        pl.semaphore_signal(barrier, inc=1, device_id=(dp, partners[k]), device_id_type=MESH)
    for other in (sibling, across):
        pl.semaphore_signal(barrier, inc=1, device_id=(other, me), device_id_type=MESH)

    before = (
        lax.broadcasted_iota(jnp.int32, (slots, slots), 0)
        < lax.broadcasted_iota(jnp.int32, (slots, slots), 1)
    ).astype(F32).astype(BF16)
    held = owner_ref[...] == me
    code_ref[...] = jnp.where(held, dot(held.astype(F32).astype(BF16), before), -1.0)
    line = lax.broadcasted_iota(jnp.int32, (slab, 1), 0)
    level = jnp.where(line < cap, line, line - cap).astype(F32)
    first = line < cap
    spots = lax.broadcasted_iota(jnp.int32, (tokens_here, 1), 0)
    for k in ORDER + (0,):
        wanted = code_ref[pl.ds(partners[k], 1), :]
        at_level = (wanted == level).astype(F32).astype(BF16)
        at_row = (row_ref[pl.ds(partners[k], 1), :] == spots).astype(F32).astype(BF16)
        chosen = contract_last(at_level, at_row)
        sel[pl.ds(k * slab, slab), pl.ds(0, tokens_here)] = jnp.where(first, chosen, 0.0).astype(BF16)
        sel[pl.ds(k * slab, slab), pl.ds(tokens_here, tokens_here)] = jnp.where(
            first, 0.0, chosen
        ).astype(BF16)

    pl.semaphore_wait(barrier, peers - 1 + 2)

    copies = []
    forward = {}
    for which, table in ((0, tt), (1, cc)):
        loads[2 * which].wait()
        loads[2 * which + 1].wait()
        for k in ORDER + (0,):
            for piece in range(0, half, 512):
                picked = dot(
                    sel[pl.ds(k * slab, slab), :], table[:, pl.ds(piece, 512)]
                ).astype(BF16)
                if k:
                    send[which, k, :, pl.ds(piece, 512)] = picked
                else:
                    got[which, k, :, pl.ds(piece, 512)] = picked
            if k:
                copy = pltpu.make_async_remote_copy(
                    src_ref=send.at[which, k],
                    dst_ref=got.at[which, k],
                    send_sem=send_sem.at[which, k],
                    recv_sem=recv_sem.at[which, k],
                    device_id=(dp, partners[k]),
                    device_id_type=MESH,
                )
                copy.start()
                copies.append(copy)
                forward[which, k] = copy

    own_owner = owner_ref[pl.ds(me, 1), :]
    owned = own_owner == lax.broadcasted_iota(jnp.int32, (peers, 1), 0)
    ranks = dot(owned.astype(F32).astype(BF16), before)
    own_rank = jnp.sum(jnp.where(owned, ranks, 0.0), axis=0, keepdims=True)
    for k in range(peers):
        hit = ((own_owner == partners[k]) & (own_rank == level)).astype(F32)
        left, right = jnp.where(first, hit, 0.0), jnp.where(first, 0.0, hit)
        put[pl.ds(k * slab, slab), pl.ds(0, slots)] = left.astype(BF16)
        put[pl.ds(k * slab, slab), pl.ds(slots, slots)] = right.astype(BF16)
    for part in range(0, peers * slab, 128):
        take[:, pl.ds(part, 128)] = put[pl.ds(part, 128), :].astype(F32).T.astype(BF16)
    weight = jnp.broadcast_to(gates_ref[...], (128, slots)).T[:, :1]
    for number in (4, 5, 6):
        loads[number].wait()

    def pick(which):
        for k in ORDER:
            forward[which, k].wait_recv()
        flat = got.at[which].reshape(peers * slab, half)

        for piece in range(0, half, 256):
            picked = dot(take[...], flat[:, pl.ds(piece, 256)]).astype(BF16)
            rows[which, :, pl.ds(piece, 256)] = picked[:slots]
            rows[which, :, pl.ds(half + piece, 256)] = picked[slots:]

    pick(0)
    pre[...] = dot(rows[0], wgu[...])
    pick(1)
    raw = contract_last(rows[1], wd[...])
    pre_gate = pre[:, :ff]
    pre_up = pre[:, ff:]
    sigma = jax.nn.sigmoid(pre_gate)
    activated = pre_gate * sigma
    hidden = activated * pre_up
    gate_rows = jnp.sum(hidden * raw, axis=1, keepdims=True)
    gr_out[...] = jnp.broadcast_to(gate_rows, (slots, 128)).T[:1]
    hid[...] = (hidden * weight).astype(BF16)
    d_hidden = raw * weight
    dpre[:, :ff] = (d_hidden * pre_up * sigma * (1.0 + pre_gate * (1.0 - sigma))).astype(BF16)
    dpre[:, ff:] = (d_hidden * activated).astype(BF16)

    for piece in range(0, half, 512):
        for side in range(2):
            grad = contract_last(dpre[...], wgu[pl.ds(side * half + piece, 512), :])
            outg[pl.ds(side * slots, slots), pl.ds(piece, 512)] = grad.astype(BF16)
    backward = {}
    for k in ORDER + (0,):
        for piece in range(0, half, 512):
            placed = dot(
                put[pl.ds(k * slab, slab), :], outg[:, pl.ds(piece, 512)]
            ).astype(BF16)
            if k:
                back_send[k, :, pl.ds(piece, 512)] = placed
            else:
                back_got[k, :, pl.ds(piece, 512)] = placed
        if k:
            copy = pltpu.make_async_remote_copy(
                src_ref=back_send.at[k],
                dst_ref=back_got.at[k],
                send_sem=bsend_sem.at[k],
                recv_sem=brecv_sem.at[k],
                device_id=(dp, partners[k]),
                device_id_type=MESH,
            )
            copy.start()
            copies.append(copy)
            backward[k] = copy

    def parts(owner):
        columns = pl.ds(pl.multiple_of(owner * shard, shard), shard)
        return (
            contract_first(rows[0, :, columns], dpre[...]),
            contract_first(hid[...], rows[1, :, columns]),
        )

    planes = (1 - plane, plane)
    core_copies = {}
    for j in range(2):
        one, two = parts(planes[j] * 2 + (1 - core))
        core_send_a[j] = one.astype(BF16)
        core_send_b[j] = two.astype(BF16)
        for n, (src, dst) in enumerate(((core_send_a, core_got_a), (core_send_b, core_got_b))):
            copy = pltpu.make_async_remote_copy(
                src_ref=src.at[j],
                dst_ref=dst.at[j],
                send_sem=csend_sem.at[j, n],
                recv_sem=crecv_sem.at[j, n],
                device_id=(sibling, me),
                device_id_type=MESH,
            )
            copy.start()
            copies.append(copy)
            core_copies[j, n] = copy
        one, two = parts(planes[j] * 2 + core)
        own_a[j] = one
        own_b[j] = two
        if j == 0:
            x_copies = []
            for n, (own, near, src, dst) in enumerate((
                (own_a, core_got_a, x_send_a, x_got_a),
                (own_b, core_got_b, x_send_b, x_got_b),
            )):
                core_copies[0, n].wait_recv()
                src[...] = (own[0] + near[0].astype(F32)).astype(BF16)
                copy = pltpu.make_async_remote_copy(
                    src_ref=src,
                    dst_ref=dst,
                    send_sem=xsend_sem.at[n],
                    recv_sem=xrecv_sem.at[n],
                    device_id=(across, me),
                    device_id_type=MESH,
                )
                copy.start()
                copies.append(copy)
                x_copies.append(copy)
    core_copies[1, 0].wait_recv()
    own_a[1] = own_a[1] + core_got_a[1].astype(F32)
    core_copies[1, 1].wait_recv()
    own_b[1] = own_b[1] + core_got_b[1].astype(F32)

    x_copies[0].wait_recv()
    total = own_a[1] + x_got_a[...].astype(F32)
    gg_out[...] = total[:, :ff]
    gu_out[...] = total[:, ff:]
    x_copies[1].wait_recv()
    gd_out[...] = own_b[1] + x_got_b[...].astype(F32)

    for k in ORDER:
        backward[k].wait_recv()
    flat_back = back_got.reshape(peers * slab, half)
    for piece in range(0, half, 256):
        summed = contract_first(sel[...], flat_back[:, pl.ds(piece, 256)]).astype(BF16)
        tg_out[:, pl.ds(piece, 256)] = summed[:tokens_here]
        tg_out[:, pl.ds(half + piece, 256)] = summed[tokens_here:]
    for copy in copies:
        copy.wait_send()


def by_kernel(cap, tokens, cotangent, w_gate, w_up, w_down, route_owner, route_row, gates):
    peers = route_owner.shape[1]
    slots = route_owner.shape[2]
    tokens_here, width = tokens.shape[1:]
    ff = w_gate.shape[2]
    half, shard, slab = width // 2, width // 4, 2 * cap
    vmem = pl.BlockSpec(memory_space=pltpu.VMEM)
    hbm = pl.BlockSpec(memory_space=pl.ANY)
    dma = pltpu.SemaphoreType.DMA
    outs = pl.pallas_call(
        functools.partial(fused, peers, cap),
        out_shape=(
            jax.ShapeDtypeStruct((tokens_here, width), BF16),
            jax.ShapeDtypeStruct((shard, ff), F32),
            jax.ShapeDtypeStruct((shard, ff), F32),
            jax.ShapeDtypeStruct((ff, shard), F32),
            jax.ShapeDtypeStruct((1, slots), F32),
        ),
        in_specs=[hbm] * 5 + [vmem] * 3,
        out_specs=(vmem,) * 5,
        scratch_shapes=[
            pltpu.VMEM((2 * tokens_here, half), BF16),
            pltpu.VMEM((2 * tokens_here, half), BF16),
            pltpu.VMEM((width, 2 * ff), BF16),
            pltpu.VMEM((ff, width), BF16),
            pltpu.VMEM((peers, slots), F32),
            pltpu.VMEM((peers * slab, 2 * tokens_here), BF16),
            pltpu.VMEM((peers * slab, 2 * slots), BF16),
            pltpu.VMEM((2 * slots, peers * slab), BF16),
            pltpu.VMEM((2, peers, slab, half), BF16),
            pltpu.VMEM((2, peers, slab, half), BF16),
            pltpu.VMEM((peers, slab, half), BF16),
            pltpu.VMEM((peers, slab, half), BF16),
            pltpu.VMEM((2, slots, width), BF16),
            pltpu.VMEM((slots, 2 * ff), F32),
            pltpu.VMEM((slots, 2 * ff), BF16),
            pltpu.VMEM((slots, ff), BF16),
            pltpu.VMEM((2 * slots, half), BF16),
            pltpu.VMEM((2, shard, 2 * ff), BF16),
            pltpu.VMEM((2, shard, 2 * ff), BF16),
            pltpu.VMEM((2, shard, 2 * ff), F32),
            pltpu.VMEM((shard, 2 * ff), BF16),
            pltpu.VMEM((shard, 2 * ff), BF16),
            pltpu.VMEM((2, ff, shard), BF16),
            pltpu.VMEM((2, ff, shard), BF16),
            pltpu.VMEM((2, ff, shard), F32),
            pltpu.VMEM((ff, shard), BF16),
            pltpu.VMEM((ff, shard), BF16),
            dma((7,)),
            dma((2, peers)),
            dma((2, peers)),
            dma((peers,)),
            dma((peers,)),
            dma((2, 2)),
            dma((2, 2)),
            dma((2,)),
            dma((2,)),
        ],
        compiler_params=pltpu.CompilerParams(
            collective_id=0, has_side_effects=True, vmem_limit_bytes=56 * 1024 * 1024
        ),
        name="moe_backward",
    )(
        tokens[0], cotangent[0], w_gate[0], w_up[0], w_down[0],
        route_owner[0], route_row[0], gates[0],
    )
    token_grads, gate_sum, up_sum, down_sum, gate_rows = outs
    return token_grads[None], gate_sum[None], up_sum[None], down_sum[None], gate_rows[None]


def on_device_any(tokens, cotangent, w_gate, w_up, w_down, route_owner, route_row, gates):
    peers = lax.axis_size("expert")
    slots = route_owner.shape[2]
    cap = (5 * slots + 4 * peers - 1) // (4 * peers)
    arrays = (tokens, cotangent, w_gate, w_up, w_down, route_owner, route_row, gates)
    if peers == 8 and lax.axis_size("dp") == 4 and cap % 8 == 0:
        return by_kernel(cap, *arrays)
    return on_device(*arrays)


def solution(mesh):
    return jax.shard_map(
        on_device_any,
        mesh=mesh,
        in_specs=(
            P("dp", "expert", None),
            P("dp", "expert", None),
            P("expert", None, None),
            P("expert", None, None),
            P("expert", None, None),
            P("dp", None, None),
            P("dp", None, None),
            P("dp", "expert", None),
        ),
        out_specs=(
            P("dp", "expert", None),
            P("expert", "dp", None),
            P("expert", "dp", None),
            P("expert", None, "dp"),
            P("dp", "expert", None),
        ),
        check_vma=False,
    )
```

```python
import functools

import jax
import jax.numpy as jnp
from jax import lax
from jax.experimental import pallas as pl
from jax.experimental.pallas import tpu as pltpu
from jax.sharding import PartitionSpec as P


def contract_first(left, right):
    return lax.dot_general(
        left, right, (((0,), (0,)), ((), ())), preferred_element_type=jnp.float32
    )


def contract_last(left, right):
    return lax.dot_general(
        left, right, (((1,), (1,)), ((), ())), preferred_element_type=jnp.float32
    )


def on_device(tokens, cotangent, w_gate, w_up, w_down, route_owner, route_row, gates):
    peers = lax.axis_size("expert")
    device = lax.axis_index("expert")
    local_tokens = tokens[0]
    local_cotangent = cotangent[0]
    gate_matrix = w_gate[0]
    up_matrix = w_up[0]
    down_matrix = w_down[0]
    owners_all = route_owner[0]
    rows_all = route_row[0]
    token_count = local_tokens.shape[0]
    width = local_tokens.shape[1]
    slots_each = owners_all.shape[1]
    capacity = (5 * slots_each + 4 * peers - 1) // (4 * peers)
    held_here = owners_all == device
    ranks_here = jnp.cumsum(held_here.astype(jnp.int32), axis=1) - 1
    levels = jnp.arange(capacity, dtype=jnp.int32)
    matches = held_here[None, :, :] & (ranks_here[None, :, :] == levels[:, None, None])
    wanted_by_level = jnp.sum(jnp.where(matches, rows_all[None, :, :] + 1, 0), axis=2) - 1
    wanted = wanted_by_level.T.reshape(-1)
    selector = (wanted[:, None] == jnp.arange(token_count, dtype=jnp.int32)[None, :]).astype(
        jnp.bfloat16
    )
    send_inputs = jnp.dot(selector, local_tokens, preferred_element_type=jnp.float32).astype(
        jnp.bfloat16
    )
    send_outputs = jnp.dot(selector, local_cotangent, preferred_element_type=jnp.float32).astype(
        jnp.bfloat16
    )
    got_inputs = lax.all_to_all(
        send_inputs.reshape(peers, capacity * width),
        "expert",
        split_axis=0,
        concat_axis=0,
        tiled=True,
    )
    got_outputs = lax.all_to_all(
        send_outputs.reshape(peers, capacity * width),
        "expert",
        split_axis=0,
        concat_axis=0,
        tiled=True,
    )
    own_owner = lax.dynamic_index_in_dim(owners_all, device, 0, keepdims=False)
    own_gate = gates[0, 0]
    owner_hits = (own_owner[:, None] == jnp.arange(peers, dtype=jnp.int32)[None, :]).astype(
        jnp.int32
    )
    own_rank = jnp.sum(owner_hits * (jnp.cumsum(owner_hits, axis=0) - 1), axis=1)
    slot_index = own_owner * capacity + own_rank
    flat_inputs = got_inputs.reshape(peers * capacity, width)
    flat_outputs = got_outputs.reshape(peers * capacity, width)
    rows_in = jnp.take(flat_inputs, slot_index, axis=0)
    rows_out = jnp.take(flat_outputs, slot_index, axis=0)
    pre_gate = jnp.dot(rows_in, gate_matrix, preferred_element_type=jnp.float32)
    pre_up = jnp.dot(rows_in, up_matrix, preferred_element_type=jnp.float32)
    sigma = jax.nn.sigmoid(pre_gate)
    activated = pre_gate * sigma
    hidden = (activated * pre_up).astype(jnp.bfloat16)
    expert_out = jnp.dot(hidden, down_matrix, preferred_element_type=jnp.float32)
    gate_grad_rows = jnp.sum(rows_out.astype(jnp.float32) * expert_out, axis=1)
    scaled = (own_gate[:, None] * rows_out.astype(jnp.float32)).astype(jnp.bfloat16)
    d_hidden = contract_last(scaled, down_matrix)
    d_pre_gate = (d_hidden * pre_up * sigma * (1.0 + pre_gate * (1.0 - sigma))).astype(jnp.bfloat16)
    d_pre_up = (d_hidden * activated).astype(jnp.bfloat16)
    row_grad = (contract_last(d_pre_gate, gate_matrix) + contract_last(d_pre_up, up_matrix)).astype(
        jnp.bfloat16
    )
    gate_part = contract_first(rows_in, d_pre_gate)
    up_part = contract_first(rows_in, d_pre_up)
    down_part = contract_first(scaled, hidden)
    gate_sum, up_sum, down_sum = (
        lax.psum_scatter(
            gate_part.astype(jnp.bfloat16), "dp", scatter_dimension=0, tiled=True
        ).astype(jnp.float32),
        lax.psum_scatter(
            up_part.astype(jnp.bfloat16), "dp", scatter_dimension=0, tiled=True
        ).astype(jnp.float32),
        lax.psum_scatter(
            down_part.astype(jnp.bfloat16), "dp", scatter_dimension=0, tiled=True
        ).astype(jnp.float32),
    )
    back_rows = jnp.zeros((peers * capacity, width), jnp.bfloat16).at[slot_index].set(row_grad)
    got_back = lax.all_to_all(
        back_rows.reshape(peers, capacity * width),
        "expert",
        split_axis=0,
        concat_axis=0,
        tiled=True,
    )
    token_grads = contract_first(selector, got_back.reshape(peers * capacity, width)).astype(
        jnp.bfloat16
    )
    return (
        token_grads[None],
        gate_sum[None],
        up_sum[None],
        down_sum.T[None],
        gate_grad_rows[None, None],
    )


MESH = pl.DeviceIdType.MESH
F32 = jnp.float32
BF16 = jnp.bfloat16
ORDER = (6, 7, 4, 5, 2, 3, 1)


def flipped(index, bits, size):
    out = 0
    step = 1
    while step < size:
        out = out + step * (((index // step) % 2 + (bits // step) % 2) % 2)
        step *= 2
    return out


def dot(left, right):
    return jnp.dot(left, right, preferred_element_type=F32)


def fused(
    peers, cap, tok_hbm, cot_hbm, wg_hbm, wu_hbm, wd_hbm, owner_ref, row_ref, gates_ref,
    tg_out, own_a_out, x_got_a, own_b_out, x_got_b, gr_out,
    tt, cc, wgu, wd, code_ref, sel, put, take, send, got, back_send, back_got,
    sel_t, tg, rows, pre, dpre, hid, outg,
    core_send_a, core_got_a, own_a, x_send_a,
    core_send_b, core_got_b, own_b, x_send_b,
    load_sem, send_sem, recv_sem, bsend_sem, brecv_sem, csend_sem, crecv_sem, xsend_sem, xrecv_sem, store_sem,
):
    me = lax.axis_index("expert")
    dp = lax.axis_index("dp")
    plane, core = dp // 2, dp % 2
    sibling = plane * 2 + (1 - core)
    across = (1 - plane) * 2 + core
    tokens_here, width = tok_hbm.shape
    half = width // 2
    slots = owner_ref.shape[1]
    ff = wg_hbm.shape[1]
    shard = width // 4
    slab = 2 * cap
    partners = {k: flipped(me, k, peers) for k in range(peers)}

    loads = []
    for number, (src, dst) in enumerate((
        (tok_hbm.at[:, pl.ds(0, half)], tt.at[pl.ds(0, tokens_here)]),
        (tok_hbm.at[:, pl.ds(half, half)], tt.at[pl.ds(tokens_here, tokens_here)]),
        (cot_hbm.at[:, pl.ds(0, half)], cc.at[pl.ds(0, tokens_here)]),
        (cot_hbm.at[:, pl.ds(half, half)], cc.at[pl.ds(tokens_here, tokens_here)]),
        (wg_hbm, wgu.at[:, pl.ds(0, ff)]),
        (wu_hbm, wgu.at[:, pl.ds(ff, ff)]),
        (wd_hbm, wd),
    )):
        copy = pltpu.make_async_copy(src, dst, load_sem.at[number])
        copy.start()
        loads.append(copy)

    barrier = pltpu.get_barrier_semaphore()
    for k in ORDER:
        pl.semaphore_signal(barrier, inc=1, device_id=(dp, partners[k]), device_id_type=MESH)
    for other in (sibling, across):
        pl.semaphore_signal(barrier, inc=1, device_id=(other, me), device_id_type=MESH)

    before = (
        lax.broadcasted_iota(jnp.int32, (slots, slots), 0)
        < lax.broadcasted_iota(jnp.int32, (slots, slots), 1)
    ).astype(F32).astype(BF16)
    held = owner_ref[...] == me
    code_ref[...] = jnp.where(held, dot(held.astype(F32).astype(BF16), before), -1.0)
    line = lax.broadcasted_iota(jnp.int32, (slab, 1), 0)
    level = jnp.where(line < cap, line, line - cap).astype(F32)
    first = line < cap
    spots = lax.broadcasted_iota(jnp.int32, (tokens_here, 1), 0)
    def choose(k):
        wanted = code_ref[pl.ds(partners[k], 1), :]
        at_level = (wanted == level).astype(F32).astype(BF16)
        at_row = (row_ref[pl.ds(partners[k], 1), :] == spots).astype(F32).astype(BF16)
        chosen = contract_last(at_level, at_row)
        sel[pl.ds(k * slab, slab), pl.ds(0, tokens_here)] = jnp.where(first, chosen, 0.0).astype(BF16)
        sel[pl.ds(k * slab, slab), pl.ds(tokens_here, tokens_here)] = jnp.where(
            first, 0.0, chosen
        ).astype(BF16)

    copies = []
    forward = {}
    for which, table in ((0, tt), (1, cc)):
        for k in ORDER + (0,):
            if which == 0:
                choose(k)
            if k == ORDER[0]:
                loads[2 * which].wait()
                loads[2 * which + 1].wait()
            for piece in range(0, half, 512):
                picked = dot(
                    sel[pl.ds(k * slab, slab), :], table[:, pl.ds(piece, 512)]
                ).astype(BF16)
                if k:
                    send[which, k, :, pl.ds(piece, 512)] = picked
                else:
                    got[which, k, :, pl.ds(piece, 512)] = picked
            if which == 0 and k == ORDER[0]:
                pl.semaphore_wait(barrier, peers - 1 + 2)
            if k:
                copy = pltpu.make_async_remote_copy(
                    src_ref=send.at[which, k],
                    dst_ref=got.at[which, k],
                    send_sem=send_sem.at[which, k],
                    recv_sem=recv_sem.at[which, k],
                    device_id=(dp, partners[k]),
                    device_id_type=MESH,
                )
                copy.start()
                copies.append(copy)
                forward[which, k] = copy

    own_owner = owner_ref[pl.ds(me, 1), :]
    owned = own_owner == lax.broadcasted_iota(jnp.int32, (peers, 1), 0)
    ranks = dot(owned.astype(F32).astype(BF16), before)
    own_rank = jnp.sum(jnp.where(owned, ranks, 0.0), axis=0, keepdims=True)
    for k in range(peers):
        hit = ((own_owner == partners[k]) & (own_rank == level)).astype(F32)
        left, right = jnp.where(first, hit, 0.0), jnp.where(first, 0.0, hit)
        put[pl.ds(k * slab, slab), pl.ds(0, slots)] = left.astype(BF16)
        put[pl.ds(k * slab, slab), pl.ds(slots, slots)] = right.astype(BF16)
    for part in range(0, peers * slab, 128):
        take[:, pl.ds(part, 128)] = put[pl.ds(part, 128), :].astype(F32).T.astype(BF16)
        sel_t[:, pl.ds(part, 128)] = sel[pl.ds(part, 128), :].astype(F32).T.astype(BF16)
    weight = jnp.broadcast_to(gates_ref[...], (128, slots)).T[:, :1]
    for number in (4, 5, 6):
        loads[number].wait()

    def pick(which):
        for k in ORDER:
            forward[which, k].wait_recv()
        flat = got.at[which].reshape(peers * slab, half)

        for piece in range(0, half, 256):
            picked = dot(take[...], flat[:, pl.ds(piece, 256)]).astype(BF16)
            rows[which, :, pl.ds(piece, 256)] = picked[:slots]
            rows[which, :, pl.ds(half + piece, 256)] = picked[slots:]

    planes = (1 - plane, plane)
    core_copies = {}
    x_copies = {}
    stores = []

    def part(n, j, core_of):
        columns = pl.ds(pl.multiple_of((planes[j] * 2 + core_of) * shard, shard), shard)
        if n == 0:
            return contract_first(rows[0, :, columns], dpre[...])
        return contract_first(hid[...], rows[1, :, columns])

    sums = (
        (core_send_a, core_got_a, own_a, x_send_a, x_got_a, own_a_out),
        (core_send_b, core_got_b, own_b, x_send_b, x_got_b, own_b_out),
    )

    def to_core(n, j):
        src, dst = sums[n][:2]
        src[j] = part(n, j, 1 - core).astype(BF16)
        copy = pltpu.make_async_remote_copy(
            src_ref=src.at[j],
            dst_ref=dst.at[j],
            send_sem=csend_sem.at[j, n],
            recv_sem=crecv_sem.at[j, n],
            device_id=(sibling, me),
            device_id_type=MESH,
        )
        copy.start()
        copies.append(copy)
        core_copies[j, n] = copy

    def keep(n, j):
        sums[n][2][j] = part(n, j, core)

    def to_plane(n):
        _, near, own, src, dst, _ = sums[n]
        core_copies[0, n].wait_recv()
        src[...] = (own[0] + near[0].astype(F32)).astype(BF16)
        copy = pltpu.make_async_remote_copy(
            src_ref=src,
            dst_ref=dst,
            send_sem=xsend_sem.at[n],
            recv_sem=xrecv_sem.at[n],
            device_id=(across, me),
            device_id_type=MESH,
        )
        copy.start()
        copies.append(copy)
        x_copies[n] = copy

    def store(src, dst):
        copy = pltpu.make_async_copy(src, dst, store_sem.at[len(stores)])
        copy.start()
        stores.append(copy)

    def finish(n):
        _, near, own, _, _, out = sums[n]
        core_copies[1, n].wait_recv()
        own[1] = own[1] + near[1].astype(F32)
        store(own.at[1], out)

    pick(0)
    pre[...] = dot(rows[0], wgu[...])
    pre_gate = pre[:, :ff]
    hid[...] = (pre_gate * jax.nn.sigmoid(pre_gate) * pre[:, ff:] * weight).astype(BF16)

    pick(1)
    to_core(1, 0)
    raw = contract_last(rows[1], wd[...])
    pre_gate = pre[:, :ff]
    pre_up = pre[:, ff:]
    sigma = jax.nn.sigmoid(pre_gate)
    activated = pre_gate * sigma
    d_hidden = raw * weight
    dpre[:, :ff] = (d_hidden * pre_up * sigma * (1.0 + pre_gate * (1.0 - sigma))).astype(BF16)
    dpre[:, ff:] = (d_hidden * activated).astype(BF16)
    gate_rows = jnp.sum(activated * pre_up * raw, axis=1, keepdims=True)
    gr_out[...] = jnp.broadcast_to(gate_rows, (slots, 128)).T[:1]
    keep(1, 0)
    to_plane(1)

    for piece in range(0, half, 512):
        for side in range(2):
            grad = contract_last(dpre[...], wgu[pl.ds(side * half + piece, 512), :])
            outg[pl.ds(side * slots, slots), pl.ds(piece, 512)] = grad.astype(BF16)
    backward = {}

    def give_back(k):
        for piece in range(0, half, 512):
            placed = dot(
                put[pl.ds(k * slab, slab), :], outg[:, pl.ds(piece, 512)]
            ).astype(BF16)
            if k:
                back_send[k, :, pl.ds(piece, 512)] = placed
            else:
                back_got[k, :, pl.ds(piece, 512)] = placed
        if k:
            copy = pltpu.make_async_remote_copy(
                src_ref=back_send.at[k],
                dst_ref=back_got.at[k],
                send_sem=bsend_sem.at[k],
                recv_sem=brecv_sem.at[k],
                device_id=(dp, partners[k]),
                device_id_type=MESH,
            )
            copy.start()
            copies.append(copy)
            backward[k] = copy

    for k in ORDER[:4]:
        give_back(k)
    to_core(0, 0)
    for k in ORDER[4:] + (0,):
        give_back(k)
    keep(0, 0)
    to_plane(0)
    for n in (1, 0):
        to_core(n, 1)
        keep(n, 1)
    finish(1)
    finish(0)

    for k in ORDER:
        backward[k].wait_recv()
    flat_back = back_got.reshape(peers * slab, half)
    for piece in range(0, half, 256):
        summed = dot(sel_t[...], flat_back[:, pl.ds(piece, 256)]).astype(BF16)
        tg[:, pl.ds(piece, 256)] = summed[:tokens_here]
        tg[:, pl.ds(half + piece, 256)] = summed[tokens_here:]
    store(tg, tg_out)
    x_copies[1].wait_recv()
    x_copies[0].wait_recv()
    for copy in copies:
        copy.wait_send()
    for copy in stores:
        copy.wait()


def by_kernel(cap, tokens, cotangent, w_gate, w_up, w_down, route_owner, route_row, gates):
    peers = route_owner.shape[1]
    slots = route_owner.shape[2]
    tokens_here, width = tokens.shape[1:]
    ff = w_gate.shape[2]
    half, shard, slab = width // 2, width // 4, 2 * cap
    vmem = pl.BlockSpec(memory_space=pltpu.VMEM)
    hbm = pl.BlockSpec(memory_space=pl.ANY)
    dma = pltpu.SemaphoreType.DMA
    outs = pl.pallas_call(
        functools.partial(fused, peers, cap),
        out_shape=(
            jax.ShapeDtypeStruct((tokens_here, width), BF16),
            jax.ShapeDtypeStruct((shard, 2 * ff), F32),
            jax.ShapeDtypeStruct((shard, 2 * ff), BF16),
            jax.ShapeDtypeStruct((ff, shard), F32),
            jax.ShapeDtypeStruct((ff, shard), BF16),
            jax.ShapeDtypeStruct((1, slots), F32),
        ),
        in_specs=[hbm] * 5 + [vmem] * 3,
        out_specs=(hbm,) * 5 + (vmem,),
        scratch_shapes=[
            pltpu.VMEM((2 * tokens_here, half), BF16),
            pltpu.VMEM((2 * tokens_here, half), BF16),
            pltpu.VMEM((width, 2 * ff), BF16),
            pltpu.VMEM((ff, width), BF16),
            pltpu.VMEM((peers, slots), F32),
            pltpu.VMEM((peers * slab, 2 * tokens_here), BF16),
            pltpu.VMEM((peers * slab, 2 * slots), BF16),
            pltpu.VMEM((2 * slots, peers * slab), BF16),
            pltpu.VMEM((2, peers, slab, half), BF16),
            pltpu.VMEM((2, peers, slab, half), BF16),
            pltpu.VMEM((peers, slab, half), BF16),
            pltpu.VMEM((peers, slab, half), BF16),
            pltpu.VMEM((2 * tokens_here, peers * slab), BF16),
            pltpu.VMEM((tokens_here, width), BF16),
            pltpu.VMEM((2, slots, width), BF16),
            pltpu.VMEM((slots, 2 * ff), F32),
            pltpu.VMEM((slots, 2 * ff), BF16),
            pltpu.VMEM((slots, ff), BF16),
            pltpu.VMEM((2 * slots, half), BF16),
            pltpu.VMEM((2, shard, 2 * ff), BF16),
            pltpu.VMEM((2, shard, 2 * ff), BF16),
            pltpu.VMEM((2, shard, 2 * ff), F32),
            pltpu.VMEM((shard, 2 * ff), BF16),
            pltpu.VMEM((2, ff, shard), BF16),
            pltpu.VMEM((2, ff, shard), BF16),
            pltpu.VMEM((2, ff, shard), F32),
            pltpu.VMEM((ff, shard), BF16),
            dma((7,)),
            dma((2, peers)),
            dma((2, peers)),
            dma((peers,)),
            dma((peers,)),
            dma((2, 2)),
            dma((2, 2)),
            dma((2,)),
            dma((2,)),
            dma((3,)),
        ],
        compiler_params=pltpu.CompilerParams(
            collective_id=0, has_side_effects=True, vmem_limit_bytes=56 * 1024 * 1024
        ),
        name="moe_backward",
    )(
        tokens[0], cotangent[0], w_gate[0], w_up[0], w_down[0],
        route_owner[0], route_row[0], gates[0],
    )
    token_grads, own_a, got_a, own_b, got_b, gate_rows = outs
    return (
        token_grads[None],
        (own_a[:, :ff] + got_a[:, :ff].astype(F32))[None],
        (own_a[:, ff:] + got_a[:, ff:].astype(F32))[None],
        (own_b + got_b.astype(F32))[None],
        gate_rows[None],
    )


def on_device_any(tokens, cotangent, w_gate, w_up, w_down, route_owner, route_row, gates):
    peers = lax.axis_size("expert")
    slots = route_owner.shape[2]
    cap = (5 * slots + 4 * peers - 1) // (4 * peers)
    arrays = (tokens, cotangent, w_gate, w_up, w_down, route_owner, route_row, gates)
    if peers == 8 and lax.axis_size("dp") == 4 and cap % 8 == 0:
        return by_kernel(cap, *arrays)
    return on_device(*arrays)


def solution(mesh):
    return jax.shard_map(
        on_device_any,
        mesh=mesh,
        in_specs=(
            P("dp", "expert", None),
            P("dp", "expert", None),
            P("expert", None, None),
            P("expert", None, None),
            P("expert", None, None),
            P("dp", None, None),
            P("dp", None, None),
            P("dp", "expert", None),
        ),
        out_specs=(
            P("dp", "expert", None),
            P("expert", "dp", None),
            P("expert", "dp", None),
            P("expert", None, "dp"),
            P("dp", "expert", None),
        ),
        check_vma=False,
    )
```
